32 devices in a mesh: group: 1, expert: 32 (over z, y, x, core).
Axes of the slice: x: 2, y: 2, z: 4, core: 2. Of those that a mesh axis runs over, the one named last changes fastest.
Arguments:
- tokens: bfloat16 [1024, 2048], P(('group', 'expert')), may hold values from -6 to 6
- upstream: bfloat16 [1024, 2048], P(('group', 'expert')), may hold values from -6 to 6
- expert_ids: int32 [1024, 8], P(('group', 'expert')), may hold values from 0 to 15, all different within a row; in each aligned block of 32 rows (0 to 31, 32 to 63, ...) at most 24 rows name the same one
- gate_weights: bfloat16 [1024, 8], P(('group', 'expert')), may hold values from 0.049804688 to 1
- w_gate: bfloat16 [2048, 12288], P('group', 'expert'), may hold values from -0.125 to 0.125
- w_up: bfloat16 [2048, 12288], P('group', 'expert'), may hold values from -0.125 to 0.125
- w_down: bfloat16 [12288, 2048], P('expert', 'group'), may hold values from -0.21875 to 0.21875
Outputs:
- grad_tokens: bfloat16 [1024, 2048], P(('group', 'expert'))
- grad_gates: bfloat16 [1024, 8], P(('group', 'expert'))
- grad_w_gate: bfloat16 [2048, 12288], P('group', 'expert')
- grad_w_up: bfloat16 [2048, 12288], P('group', 'expert')
- grad_w_down: bfloat16 [12288, 2048], P('expert', 'group')
The draws below stay inside these ranges and needn't reach their ends.
Inputs may be any that keep to these rules, and one draw needn't show every extreme that they name: `expert_ids`: each token names 8 different experts. Within the 32 tokens of one index of expert, no expert is named more than 24 times, a bound that some block reaches.
All inputs are finite; a program needn't handle non-finite values.
Results may differ from the reference program's by a relative error of at most 0.0095.
Values may be sent and summed in bfloat16 or wider, within the bound.
No kernel may reach another device: no remote copies, remote signals or barrier semaphores. Data moves between devices by JAX's collectives and lax.ppermute only.
A program may use at most 128 MiB of HBM per device.

```python
import math
import jax
import jax.numpy as jnp
import numpy as np
from jax import lax

D = 2048
FW = 768
TOP = 8
TOK_DEV = 32
EXPERTS = 16
FH = 384
CAP = 24
TOKENS = 1024
N_EXPERT = 32


def block_scale(key, extent, pieces, smallest, high):
    gain = 1.0
    for dim, parts in pieces:
        steps = jax.random.uniform(jax.random.fold_in(jax.random.fold_in(key, 6), dim), (parts,), jnp.float32, smallest / len(pieces), high / len(pieces))
        gain = gain * jnp.repeat(jnp.exp(steps), extent[dim] // parts).reshape((-1,) + (1,) * (len(extent) - 1 - dim))
    return gain


def routed_block(key, own, number, rows, amount, top, bound, slope):
    ranking = jax.random.permutation(key, amount)
    heavy_load, common = portions_of(amount, rows * top, bound, slope, True), portions_of(amount, rows * top, bound, slope, False)
    places = jnp.arange(amount)

    def named(lengths, turn):
        used = int((lengths > 0).sum())
        fixed = max(1, used // 4)
        moved = fixed + (places - fixed + turn * (used - fixed)) % max(1, amount - fixed)
        return jnp.zeros((amount,), jnp.int32).at[ranking[jnp.where(places < fixed, places, moved)]].set(jnp.asarray(lengths, jnp.int32))

    lengths = jnp.where(number % 4 == 0, named(heavy_load, number // 4), named(common, number - number // 4 - 1))
    mixed = jax.random.permutation(jax.random.fold_in(own, 3), amount)
    source_of, taker = mixed[0:amount // 2 * 2:2], mixed[1:amount // 2 * 2:2]
    margin = jnp.minimum(lengths[source_of] - 1, bound - lengths[taker]) // 2
    margin = jnp.where((source_of == ranking[0]) | (taker == ranking[0]) | (lengths[taker] == 0), 0, jnp.maximum(margin, 0))
    moved = jax.random.randint(jax.random.fold_in(own, 4), (amount // 2,), 0, 1 << 20) % (margin + 1)
    lengths = lengths.at[source_of].add(-moved).at[taker].add(moved)
    members = jnp.searchsorted(jnp.cumsum(lengths), jnp.arange(rows * top), side="right").astype(jnp.int32)
    table = members.reshape(top, rows).T
    table = table[jax.random.permutation(jax.random.fold_in(own, 1), rows)]
    turn = jax.random.randint(jax.random.fold_in(own, 2), (rows, 1), 0, top)
    return jnp.take_along_axis(table, (jnp.arange(top)[None, :] + turn) % top, axis=1)


def portions_of(count, total, limit, skew, full):
    weights = [(1 << 20) // math.isqrt(standing ** skew) + 1 for standing in range(1, count + 1)]
    largest = limit if full else min(limit, max(-(-total // count), total * weights[0] // sum(weights)))
    least = 1 if total - largest >= count - 1 else 0
    holding, rest = [largest] + [least] * (count - 1), total - largest - least * (count - 1)
    while rest > 0:
        candidates = [i for i in range(1, count) if holding[i] < largest] or [i for i in range(1, count) if holding[i] < limit]
        pool, remaining = sum([weights[i] for i in candidates]), rest
        for i in candidates:
            extra = min(limit - holding[i], max(1, remaining * weights[i] // pool), rest)
            holding[i] = holding[i] + extra
            rest = rest - extra
    return np.array(holding)


def gaussian(key, shape, spread, limit, shards=(), held_as=jnp.bfloat16):
    drawn = jax.random.normal(key, shape, jnp.float32) * spread
    if len(shards) > 0:
        drawn = block_scale(key, shape, shards, -0.22, 0.18) * drawn
    return jnp.clip(drawn, min=-limit, max=limit).astype(held_as)


def setup_inputs(seed: int = 0, part: int = 0) -> dict:
    splits = jax.random.split(jax.random.key(seed), 8)
    part_splits = jax.random.split(jax.random.fold_in(splits[7], part), 8)
    tokens = gaussian(part_splits[0], (TOKENS, D), 1.0, 6.0, ((0, 32),))
    upstream = gaussian(part_splits[1], (TOKENS, D), 1.0, 6.0, ((0, 32),))
    expert_ids_keys = jax.random.split(jax.random.fold_in(part_splits[2], 1), TOKENS // TOK_DEV)
    expert_ids_turns = jax.random.permutation(jax.random.fold_in(part_splits[2], 3), TOKENS // TOK_DEV)
    expert_ids = jax.vmap(lambda own, number: routed_block(jax.random.fold_in(part_splits[2], 2), own, number, TOK_DEV, EXPERTS, TOP, CAP, 2))(expert_ids_keys, expert_ids_turns).reshape((TOKENS, TOP))
    gate_weights = jnp.clip(jnp.exp(math.log(1.0) - 2.9996462 * jax.random.uniform(part_splits[3], (TOKENS, TOP), jnp.float32) ** block_scale(part_splits[3], (TOKENS, TOP), ((0, 32),), -0.2, 0.2)), 0.049804688, 1.0).astype(jnp.bfloat16)
    w_gate = gaussian(part_splits[4], (D, EXPERTS * FW), D ** -0.5, 0.125, ((1, 32),))
    w_up = gaussian(part_splits[5], (D, EXPERTS * FW), D ** -0.5, 0.125, ((1, 32),))
    w_down = gaussian(part_splits[6], (EXPERTS * FW, D), FW ** -0.5, 0.21875, ((0, 32),))
    return {"tokens": tokens, "upstream": upstream, "expert_ids": expert_ids, "gate_weights": gate_weights, "w_gate": w_gate, "w_up": w_up, "w_down": w_down}


def half_terms(inputs, upward, gating, gate_half, up_half, down_half):
    pre_gate = jnp.dot(inputs, gate_half, preferred_element_type=jnp.float32)
    pre_up = jnp.dot(inputs, up_half, preferred_element_type=jnp.float32)
    logistic = jax.nn.sigmoid(pre_gate)
    activated = pre_gate * logistic
    hidden = (activated * pre_up).astype(jnp.bfloat16)
    backward = jnp.dot(upward, down_half.T, preferred_element_type=jnp.float32)
    gate_part = jnp.sum(hidden.astype(jnp.float32) * backward, axis=1).astype(jnp.bfloat16)
    grad_hidden = gating.astype(jnp.float32)[:, None] * backward
    grad_gate = (grad_hidden * pre_up * logistic * (1.0 + pre_gate * (1.0 - logistic))).astype(jnp.bfloat16)
    grad_up = (grad_hidden * activated).astype(jnp.bfloat16)
    token_part = (jnp.dot(grad_gate, gate_half.T, preferred_element_type=jnp.float32)
                  + jnp.dot(grad_up, up_half.T, preferred_element_type=jnp.float32)).astype(jnp.bfloat16)
    return token_part, gate_part, grad_gate, grad_up, hidden


def reference(tokens, upstream, expert_ids, gate_weights, w_gate, w_up, w_down):
    per_block = TOK_DEV * TOP
    span = N_EXPERT * CAP
    block_ids = expert_ids.reshape(N_EXPERT, per_block)
    onehot = (block_ids[:, :, None] == jnp.arange(EXPERTS, dtype=jnp.int32)[None, None, :]).astype(jnp.int32)
    rank_in = jnp.sum((jnp.cumsum(onehot, axis=1) - onehot) * onehot, axis=2)
    blocks = jnp.arange(N_EXPERT, dtype=jnp.int32)[:, None]
    position = (block_ids * span + blocks * CAP + rank_in).reshape(-1).astype(jnp.int32)
    pair_index = jnp.arange(TOKENS * TOP, dtype=jnp.int32)
    slot_owner = jnp.zeros((EXPERTS * span,), jnp.int32).at[position].set(pair_index)
    filled = jnp.zeros((EXPERTS * span,), jnp.bool_).at[position].set(True)
    flat_gates = gate_weights.reshape(-1)

    def per_expert(expert):
        start = (expert * span).astype(jnp.int32)
        owners = lax.dynamic_slice_in_dim(slot_owner, start, span)
        live = lax.dynamic_slice_in_dim(filled, start, span)
        source = owners // TOP
        inputs = jnp.where(live[:, None], tokens[source], jnp.zeros((), tokens.dtype))
        upward = jnp.where(live[:, None], upstream[source], jnp.zeros((), upstream.dtype))
        gating = jnp.where(live, flat_gates[owners], jnp.zeros((), gate_weights.dtype))
        column = (expert * FW).astype(jnp.int32)
        gate_cols = lax.dynamic_slice_in_dim(w_gate, column, FW, 1)
        up_cols = lax.dynamic_slice_in_dim(w_up, column, FW, 1)
        down_rows = lax.dynamic_slice_in_dim(w_down, column, FW, 0)
        low = half_terms(inputs, upward, gating, gate_cols[:, :FH], up_cols[:, :FH], down_rows[:FH])
        high = half_terms(inputs, upward, gating, gate_cols[:, FH:], up_cols[:, FH:], down_rows[FH:])
        contribution = (low[0].astype(jnp.float32) + high[0].astype(jnp.float32)).astype(jnp.bfloat16)
        gate_grad = (low[1].astype(jnp.float32) + high[1].astype(jnp.float32)).astype(jnp.bfloat16)
        scaled = (gating.astype(jnp.float32)[:, None] * upward.astype(jnp.float32)).astype(jnp.bfloat16)
        grad_gate = jnp.concatenate([low[2], high[2]], axis=1)
        grad_up = jnp.concatenate([low[3], high[3]], axis=1)
        hidden = jnp.concatenate([low[4], high[4]], axis=1)
        grad_wg = jnp.dot(inputs.T, grad_gate, preferred_element_type=jnp.float32).astype(jnp.bfloat16)
        grad_wu = jnp.dot(inputs.T, grad_up, preferred_element_type=jnp.float32).astype(jnp.bfloat16)
        grad_wd = jnp.dot(hidden.T, scaled, preferred_element_type=jnp.float32).astype(jnp.bfloat16)
        return contribution, gate_grad, grad_wg, grad_wu, grad_wd

    results = lax.map(per_expert, jnp.arange(EXPERTS, dtype=jnp.int32))
    contributions = results[0].reshape(EXPERTS * span, D)
    gate_grads = results[1].reshape(-1)
    per_pair = contributions[position].reshape(TOKENS, TOP, D).astype(jnp.float32)
    grad_tokens = jnp.sum(per_pair, axis=1).astype(jnp.bfloat16)
    grad_gates = gate_grads[position].reshape(TOKENS, TOP)
    grad_w_gate = jnp.transpose(results[2], (1, 0, 2)).reshape(D, EXPERTS * FW)
    grad_w_up = jnp.transpose(results[3], (1, 0, 2)).reshape(D, EXPERTS * FW)
    grad_w_down = results[4].reshape(EXPERTS * FW, D)
    return grad_tokens, grad_gates, grad_w_gate, grad_w_up, grad_w_down
```

```python
import functools

import jax
import jax.numpy as jnp
from jax import lax
from jax.experimental import pallas as pl
from jax.experimental.pallas import tpu as pltpu
from jax.sharding import PartitionSpec as P

LANES = 128
PLANE = 4
VMEM_LIMIT = 56 * 1024 * 1024
F32 = jnp.float32
BF16 = jnp.bfloat16


def dot(left, right, left_axis, right_axis):
    return lax.dot_general(
        left, right, (((left_axis,), (right_axis,)), ((), ())), preferred_element_type=F32
    )


def split_index(index):
    return index >> 3, index >> 2 & 1, index >> 1 & 1, index & 1


def join_index(level, u, v, core):
    return ((level * 2 + u) * 2 + v) * 2 + core


def route(count, target):
    return [(index, join_index(*target(*split_index(index)))) for index in range(count)]


def core_route(count):
    return route(count, lambda level, u, v, core: (level, u, v, 1 - core))


def first_route(count):
    return route(
        count,
        lambda level, u, v, core: (level, u, 1 - v, core) if core == 0 else (level, 1 - u, v, core),
    )


def second_route(count):
    return route(
        count,
        lambda level, u, v, core: (level, 1 - u, v, core) if core == 0 else (level, u, 1 - v, core),
    )


def level_route(count, shift):
    levels = count // (2 * PLANE)
    return route(count, lambda level, u, v, core: ((level + shift) % levels, u, v, core))


def send(block, pairs):
    return lax.ppermute(block, "expert", pairs)


def gate_column(gates, expert):
    lane = lax.broadcasted_iota(jnp.int32, gates.shape, 1)
    return jnp.sum(jnp.where(lane == expert, gates.astype(F32), 0.0), axis=1, keepdims=True)


def terms_body(count, width, half, expert_ref, *refs):
    blocks, refs = refs[:count], refs[count:]
    weights, refs = refs[:6], refs[6:]
    parts, refs = refs[:count], refs[count:]
    hidden_ref, own_ref, other_ref, gate_w, up_w, down_w, sems = refs
    copies = []
    for side in range(2):
        span = pl.ds(side * half, half)
        copies.append(
            [
                pltpu.make_async_copy(source, place, sems.at[side * 3 + i])
                for i, (source, place) in enumerate(
                    (
                        (weights[side * 3], gate_w.at[:, span]),
                        (weights[side * 3 + 1], up_w.at[:, span]),
                        (weights[side * 3 + 2], down_w.at[span, :]),
                    )
                )
            ]
        )
    for side in copies:
        for copy in side:
            copy.start()
    expert = expert_ref[0]
    rows = jnp.concatenate([block[:, :width] for block in blocks], axis=0)
    grads = jnp.concatenate([block[:, width : 2 * width] for block in blocks], axis=0)
    gates = jnp.concatenate([block[:, 2 * width :] for block in blocks], axis=0)
    gating = gate_column(gates, expert)
    full = 2 * half
    step = 256 if full % 256 == 0 else LANES
    sums = [0.0, 0.0]
    for low in range(0, full, step):
        if low == 0:
            for copy in copies[0]:
                copy.wait()
        if low < half + step and low + step > half and low <= half:
            for copy in copies[1]:
                copy.wait()
        span = slice(low, low + step)
        pre_gate = dot(rows, gate_w[:, span], 1, 0)
        pre_up = dot(rows, up_w[:, span], 1, 0)
        backward = dot(grads, down_w[span, :], 1, 1)
        logistic = jax.nn.sigmoid(pre_gate)
        activated = pre_gate * logistic
        hidden = (activated * pre_up).astype(BF16)
        terms = hidden.astype(F32) * backward
        for part in range(0, step, LANES):
            side = 0 if low + part < half else 1
            sums[side] = sums[side] + terms[:, part : part + LANES]
        grad_hidden = gating * backward
        grad_gate = (
            grad_hidden * pre_up * logistic * (1.0 + pre_gate * (1.0 - logistic))
        ).astype(BF16)
        grad_up = (grad_hidden * activated).astype(BF16)
        hidden_ref[:, span] = hidden
        for part in range(0, step, LANES):
            at = low + part
            target, at = (own_ref, at) if at < half else (other_ref, at - half)
            target[:, at : at + LANES] = grad_gate[:, part : part + LANES]
            target[:, half + at : half + at + LANES] = grad_up[:, part : part + LANES]
    gate_grad = [jnp.sum(total, axis=1, keepdims=True).astype(BF16).astype(F32) for total in sums]
    gate_grad = gate_grad[0] + gate_grad[1]
    lane = lax.broadcasted_iota(jnp.int32, gates.shape, 1)
    gate_lanes = jnp.where(lane == expert, gate_grad, 0.0).astype(BF16)
    grad_gate = jnp.concatenate([own_ref[:, :half], other_ref[:, :half]], axis=1)
    grad_up = jnp.concatenate([own_ref[:, half:], other_ref[:, half:]], axis=1)
    start = 0
    for part in parts:
        stop = start + part.shape[0]
        part[:, width:] = gate_lanes[start:stop]
        start = stop
    wide = 512 if width % 512 == 0 else width
    for low in range(0, width, wide):
        span = slice(low, low + wide)
        token = dot(grad_gate, gate_w[span, :], 1, 1) + dot(grad_up, up_w[span, :], 1, 1)
        token = token.astype(BF16)
        start = 0
        for part in parts:
            stop = start + part.shape[0]
            part[:, span] = token[start:stop]
            start = stop


def expert_terms(blocks, weights, expert):
    width, half = weights[0].shape
    total = sum(block.shape[0] for block in blocks)
    whole = pl.BlockSpec(memory_space=pltpu.VMEM)
    count = len(blocks)
    out_shape = [jax.ShapeDtypeStruct((block.shape[0], width + LANES), BF16) for block in blocks]
    out_shape += [jax.ShapeDtypeStruct((total, 2 * half), BF16)] * 3
    results = pl.pallas_call(
        functools.partial(terms_body, count, width, half),
        out_shape=out_shape,
        in_specs=[pl.BlockSpec(memory_space=pltpu.SMEM)]
        + [whole] * count
        + [pl.BlockSpec(memory_space=pl.ANY)] * 6,
        out_specs=[whole] * len(out_shape),
        scratch_shapes=[
            pltpu.VMEM((width, 2 * half), BF16),
            pltpu.VMEM((width, 2 * half), BF16),
            pltpu.VMEM((2 * half, width), BF16),
            pltpu.SemaphoreType.DMA((6,)),
        ],
        compiler_params=pltpu.CompilerParams(vmem_limit_bytes=VMEM_LIMIT),
        cost_estimate=pl.CostEstimate(
            flops=2 * 5 * total * width * 2 * half,
            bytes_accessed=12 * width * half + 12 * total * width,
            transcendentals=total * 2 * half,
        ),
        name="expert_terms",
    )(expert, *blocks, *weights)
    return results[:count], results[count], results[count + 1], results[count + 2]


def grads_body(count, groups, half, received, expert_ref, *refs):
    rows, refs = refs[:count], refs[count:]
    grads, refs = refs[:count], refs[count:]
    gates, refs = refs[:count], refs[count:]
    hidden, refs = refs[:groups], refs[groups:]
    pairs, refs = refs[:groups], refs[groups:]
    if received:
        lent, refs = refs[:3], refs[3:]
    gate_out, up_out, down_out = refs
    join = lambda parts: jnp.concatenate([part[...] for part in parts], axis=0)
    gating = gate_column(join(gates), expert_ref[0])
    scaled = (gating * join(grads).astype(F32)).astype(BF16)
    both = dot(join(rows), join(pairs), 0, 0)
    down = dot(join(hidden), scaled, 0, 0)
    gate, up = both[:, :half], both[:, half:]
    if received:
        gate = gate + lent[0][...].astype(F32)
        up = up + lent[1][...].astype(F32)
        down = down + lent[2][...].astype(F32)
    gate_out[...] = gate.astype(BF16)
    up_out[...] = up.astype(BF16)
    down_out[...] = down.astype(BF16)


def weight_grads(blocks, hidden, pairs, side, lent, expert, width, half):
    tile = 512 if width % 512 == 0 else width
    steps = width // tile
    count, groups = len(blocks), len(hidden)
    total = sum(block.shape[0] for block in blocks)
    in_specs = [pl.BlockSpec(memory_space=pltpu.SMEM)]
    in_specs += [pl.BlockSpec((b.shape[0], tile), lambda i: (0, i)) for b in blocks]
    in_specs += [pl.BlockSpec((b.shape[0], tile), lambda i: (0, steps + i)) for b in blocks]
    in_specs += [
        pl.BlockSpec((b.shape[0], LANES), lambda i: (0, 2 * width // LANES)) for b in blocks
    ]
    in_specs += [pl.BlockSpec((h.shape[0], half), lambda i: (0, side)) for h in hidden]
    in_specs += [pl.BlockSpec((p.shape[0], 2 * half), lambda i: (0, 0)) for p in pairs]
    weight_specs = [
        pl.BlockSpec((tile, half), lambda i: (i, 0)),
        pl.BlockSpec((tile, half), lambda i: (i, 0)),
        pl.BlockSpec((half, tile), lambda i: (0, i)),
    ]
    if lent:
        in_specs += weight_specs
    return pl.pallas_call(
        functools.partial(grads_body, count, groups, half, bool(lent)),
        grid=(steps,),
        out_shape=[
            jax.ShapeDtypeStruct((width, half), BF16),
            jax.ShapeDtypeStruct((width, half), BF16),
            jax.ShapeDtypeStruct((half, width), BF16),
        ],
        in_specs=in_specs,
        out_specs=weight_specs,
        compiler_params=pltpu.CompilerParams(vmem_limit_bytes=VMEM_LIMIT),
        cost_estimate=pl.CostEstimate(
            flops=2 * 3 * total * width * half,
            bytes_accessed=4 * total * width + 6 * width * half,
            transcendentals=0,
        ),
        name="weight_grads",
    )(expert, *blocks, *blocks, *blocks, *hidden, *pairs, *lent)


def add(left, right):
    return (left.astype(F32) + right.astype(F32)).astype(BF16)


def local(tokens, upstream, expert_ids, gate_weights, w_gate, w_up, w_down):
    tok_count, width = tokens.shape
    half = w_gate.shape[1]
    count = lax.axis_size("expert")
    levels = count // (2 * PLANE)
    expert = (lax.axis_index("expert") // 2).astype(jnp.int32)[None]
    chosen = expert_ids[:, :, None] == jnp.arange(LANES, dtype=jnp.int32)[None, None, :]
    gates = jnp.sum(jnp.where(chosen, gate_weights.astype(F32)[:, :, None], 0.0), axis=1)
    home = jnp.concatenate([tokens, upstream, gates.astype(BF16)], axis=1)

    own = (w_gate, w_up, w_down)
    other = tuple(send(weight, core_route(count)) for weight in own)

    groups = [(0,)]
    for shift in range(1, levels // 2 + 1):
        groups.append((shift, levels - shift) if shift != levels - shift else (shift,))
    first, second = first_route(count), second_route(count)

    blocks_of = []
    for group in groups:
        if group == (0,):
            mine = home
        else:
            mine = [send(home, level_route(count, shift)) for shift in group]
            mine = mine[0] if len(mine) == 1 else jnp.concatenate(mine, axis=0)
        near = send(mine, first)
        beside = send(mine, second)
        across = send(beside, first)
        blocks_of.append((mine, near, beside, across))

    all_hidden, own_pairs, other_pairs, arrived = [], [], [], []
    for group, blocks in zip(groups, blocks_of):
        parts, hidden, own_pair, other_pair = expert_terms(blocks, own + other, expert)
        all_hidden.append(hidden)
        own_pairs.append(own_pair)
        other_pairs.append(other_pair)
        beside = add(parts[2], send(parts[3], first))
        near_back = send(parts[1], first)
        beside_back = send(beside, second)
        plane = parts[0].astype(F32) + near_back.astype(F32) + beside_back.astype(F32)
        plane = plane.astype(BF16)
        if group == (0,):
            arrived.append(plane)
        else:
            for i, shift in enumerate(group):
                piece = plane[i * tok_count : (i + 1) * tok_count]
                arrived.append(send(piece, level_route(count, levels - shift)))

    blocks = [block for group in blocks_of for block in group]
    lent = weight_grads(blocks, all_hidden, other_pairs, 1, (), expert, width, half)
    lent = [send(part, core_route(count)) for part in lent]
    grads = weight_grads(blocks, all_hidden, own_pairs, 0, lent, expert, width, half)

    total = sum(piece.astype(F32) for piece in arrived)
    grad_tokens = total[:, :width].astype(BF16)
    gate_sums = total[:, width:]
    grad_gates = jnp.sum(jnp.where(chosen, gate_sums[:, None, :], 0.0), axis=2).astype(BF16)
    return (grad_tokens, grad_gates, *grads)


def solution(mesh):
    rows = P(("group", "expert"), None)
    return jax.shard_map(
        local,
        mesh=mesh,
        in_specs=(rows, rows, rows, rows, P("group", "expert"), P("group", "expert"), P("expert", "group")),
        out_specs=(rows, rows, P("group", "expert"), P("group", "expert"), P("expert", "group")),
        check_vma=False,
    )
```

```python
import functools

import jax
import jax.numpy as jnp
from jax import lax
from jax.experimental import pallas as pl
from jax.experimental.pallas import tpu as pltpu
from jax.sharding import PartitionSpec as P

LANES = 128
PLANE = 4
TERMS_VMEM = 32 * 1024 * 1024
GRADS_VMEM = 40 * 1024 * 1024
F32 = jnp.float32
BF16 = jnp.bfloat16


def dot(left, right, left_axis, right_axis):
    return lax.dot_general(
        left, right, (((left_axis,), (right_axis,)), ((), ())), preferred_element_type=F32
    )


def split_index(index):
    return index >> 3, index >> 2 & 1, index >> 1 & 1, index & 1


def join_index(level, u, v, core):
    return ((level * 2 + u) * 2 + v) * 2 + core


def route(count, target):
    return [(index, join_index(*target(*split_index(index)))) for index in range(count)]


def core_route(count):
    return route(count, lambda level, u, v, core: (level, u, v, 1 - core))


def first_route(count):
    return route(
        count,
        lambda level, u, v, core: (level, u, 1 - v, core) if core == 0 else (level, 1 - u, v, core),
    )


def second_route(count):
    return route(
        count,
        lambda level, u, v, core: (level, 1 - u, v, core) if core == 0 else (level, u, 1 - v, core),
    )


def level_route(count, shift):
    levels = count // (2 * PLANE)
    return route(count, lambda level, u, v, core: ((level + shift) % levels, u, v, core))


def send(block, pairs):
    return lax.ppermute(block, "expert", pairs)


def gate_column(gates, expert):
    lane = lax.broadcasted_iota(jnp.int32, gates.shape, 1)
    return jnp.sum(jnp.where(lane == expert, gates.astype(F32), 0.0), axis=1, keepdims=True)


def terms_body(count, width, half, expert_ref, *refs):
    blocks, refs = refs[:count], refs[count:]
    gate_in, up_in, down_w, *refs = refs
    parts, refs = refs[:count], refs[count:]
    hidden_ref, pair_ref, both_w, pre_ref, sems = refs
    copies = [
        pltpu.make_async_copy(source, both_w.at[:, pl.ds(i * half, half)], sems.at[i])
        for i, source in enumerate((gate_in, up_in))
    ]
    for copy in copies:
        copy.start()
    expert = expert_ref[0]
    rows = jnp.concatenate([block[:, :width] for block in blocks], axis=0)
    grads = jnp.concatenate([block[:, width : 2 * width] for block in blocks], axis=0)
    gates = jnp.concatenate([block[:, 2 * width :] for block in blocks], axis=0)
    gating = gate_column(gates, expert)
    backward = dot(grads, down_w[...], 1, 1)
    for copy in copies:
        copy.wait()
    pre_ref[...] = dot(rows, both_w[...], 1, 0)
    total = 0.0
    for low in range(0, half, LANES):
        span = slice(low, low + LANES)
        pre_gate = pre_ref[:, span]
        pre_up = pre_ref[:, half + low : half + low + LANES]
        back = backward[:, span]
        logistic = jax.nn.sigmoid(pre_gate)
        activated = pre_gate * logistic
        hidden = (activated * pre_up).astype(BF16)
        total = total + hidden.astype(F32) * back
        grad_hidden = gating * back
        grad_gate = grad_hidden * pre_up * logistic * (1.0 + pre_gate * (1.0 - logistic))
        grad_up = grad_hidden * activated
        hidden_ref[:, span] = (gating * (activated * pre_up)).astype(BF16)
        pair_ref[:, span] = grad_gate.astype(BF16)
        pair_ref[:, half + low : half + low + LANES] = grad_up.astype(BF16)
    gate_grad = jnp.sum(total, axis=1, keepdims=True)
    lane = lax.broadcasted_iota(jnp.int32, gates.shape, 1)
    gate_lanes = jnp.where(lane == expert, gate_grad, 0.0).astype(BF16)
    scatter(gate_lanes, parts, slice(width, None))
    tile = 512 if width % 512 == 0 else width
    for low in range(0, width, tile):
        span = slice(low, low + tile)
        scatter(dot(pair_ref[...], both_w[span, :], 1, 1).astype(BF16), parts, span)


def scatter(value, parts, span):
    start = 0
    for part in parts:
        stop = start + part.shape[0]
        part[:, span] = value[start:stop]
        start = stop


def expert_terms(blocks, weights, expert):
    width, half = weights[0].shape
    total = sum(block.shape[0] for block in blocks)
    whole = pl.BlockSpec(memory_space=pltpu.VMEM)
    apart = pl.BlockSpec(memory_space=pl.ANY)
    count = len(blocks)
    out_shape = [jax.ShapeDtypeStruct((block.shape[0], width + LANES), BF16) for block in blocks]
    out_shape.append(jax.ShapeDtypeStruct((total, half), BF16))
    out_shape.append(jax.ShapeDtypeStruct((total, 2 * half), BF16))
    results = pl.pallas_call(
        functools.partial(terms_body, count, width, half),
        out_shape=out_shape,
        in_specs=[pl.BlockSpec(memory_space=pltpu.SMEM)] + [whole] * count + [apart, apart, whole],
        out_specs=[whole] * len(out_shape),
        scratch_shapes=[
            pltpu.VMEM((width, 2 * half), BF16),
            pltpu.VMEM((total, 2 * half), F32),
            pltpu.SemaphoreType.DMA((2,)),
        ],
        compiler_params=pltpu.CompilerParams(vmem_limit_bytes=TERMS_VMEM),
        cost_estimate=pl.CostEstimate(
            flops=2 * 5 * total * width * half,
            bytes_accessed=6 * width * half + 6 * total * width,
            transcendentals=total * half,
        ),
        name="expert_terms",
    )(expert, *blocks, *weights)
    return results[:count], results[count], results[count + 1]


def grads_body(count, groups, width, half, *refs):
    blocks, refs = refs[:count], refs[count:]
    hidden, refs = refs[:groups], refs[groups:]
    pairs, refs = refs[:groups], refs[groups:]
    gate_out, up_out, down_out, held, sems = refs
    tile = gate_out.shape[0]
    step, steps = pl.program_id(0), pl.num_programs(0)

    def copies(at, slot):
        start = 0
        for i, block in enumerate(blocks):
            size = block.shape[0]
            for side in range(2):
                source = pl.ds(pl.multiple_of(side * width + at * tile, LANES), tile)
                yield pltpu.make_async_copy(
                    block.at[:, source],
                    held.at[slot, side, pl.ds(start, size), :],
                    sems.at[slot, side, i],
                )
            start += size

    @pl.when(step == 0)
    def _():
        for copy in copies(0, 0):
            copy.start()

    @pl.when(step + 1 < steps)
    def _():
        for copy in copies(step + 1, (step + 1) % 2):
            copy.start()

    slot = step % 2
    for copy in copies(step, slot):
        copy.wait()
    join = lambda parts: jnp.concatenate([part[...] for part in parts], axis=0)
    rows, grads = held[slot, 0], held[slot, 1]
    both = dot(rows, join(pairs), 0, 0).astype(BF16)
    gate_out[...] = both[:, :half]
    up_out[...] = both[:, half:]
    down_out[...] = dot(join(hidden), grads, 0, 0).astype(BF16)


def weight_grads(blocks, hidden, pairs, width, half):
    count, groups = len(blocks), len(hidden)
    total = sum(block.shape[0] for block in blocks)
    tile = width // 2 if total <= 1024 else width // 8
    return pl.pallas_call(
        functools.partial(grads_body, count, groups, width, half),
        grid=(width // tile,),
        out_shape=[
            jax.ShapeDtypeStruct((width, half), BF16),
            jax.ShapeDtypeStruct((width, half), BF16),
            jax.ShapeDtypeStruct((half, width), BF16),
        ],
        in_specs=[pl.BlockSpec(memory_space=pl.ANY)] * count
        + [pl.BlockSpec(part.shape, lambda i: (0, 0)) for part in hidden + pairs],
        out_specs=[
            pl.BlockSpec((tile, half), lambda i: (i, 0)),
            pl.BlockSpec((tile, half), lambda i: (i, 0)),
            pl.BlockSpec((half, tile), lambda i: (0, i)),
        ],
        scratch_shapes=[
            pltpu.VMEM((2, 2, total, tile), BF16),
            pltpu.SemaphoreType.DMA((2, 2, count)),
        ],
        compiler_params=pltpu.CompilerParams(vmem_limit_bytes=GRADS_VMEM),
        cost_estimate=pl.CostEstimate(
            flops=2 * 3 * total * width * half,
            bytes_accessed=4 * total * width + 6 * width * half,
            transcendentals=0,
        ),
        name="weight_grads",
    )(*blocks, *hidden, *pairs)


def add(left, right):
    return (left.astype(F32) + right.astype(F32)).astype(BF16)


def local(tokens, upstream, expert_ids, gate_weights, w_gate, w_up, w_down):
    tok_count, width = tokens.shape
    half = w_gate.shape[1]
    count = lax.axis_size("expert")
    levels = count // (2 * PLANE)
    expert = (lax.axis_index("expert") // 2).astype(jnp.int32)[None]
    chosen = expert_ids[:, :, None] == jnp.arange(LANES, dtype=jnp.int32)[None, None, :]
    gates = jnp.sum(jnp.where(chosen, gate_weights.astype(F32)[:, :, None], 0.0), axis=1)
    home = jnp.concatenate([tokens, upstream, gates.astype(BF16)], axis=1)

    weights = (w_gate, w_up, w_down)
    groups = [(0,)]
    for shift in range(1, levels // 2 + 1):
        groups.append((shift, levels - shift) if shift != levels - shift else (shift,))
    first, second, swap = first_route(count), second_route(count), core_route(count)

    blocks_of = []
    for group in groups:
        if group == (0,):
            mine = home
        else:
            mine = [send(home, level_route(count, shift)) for shift in group]
            mine = mine[0] if len(mine) == 1 else jnp.concatenate(mine, axis=0)
        near = send(mine, first)
        beside = send(mine, second)
        across = send(beside, first)
        kept = [mine, near, beside, across]
        blocks_of.append(kept + [send(block, swap) for block in kept])

    all_hidden, all_pairs, arrived = [], [], []
    for group, blocks in zip(groups, blocks_of):
        parts, hidden, pair = expert_terms(blocks, weights, expert)
        all_hidden.append(hidden)
        all_pairs.append(pair)
        mine, near, beside, across = [
            add(part, send(lent, swap)) for part, lent in zip(parts[:4], parts[4:])
        ]
        beside = add(beside, send(across, first))
        near_back = send(near, first)
        beside_back = send(beside, second)
        plane = mine.astype(F32) + near_back.astype(F32) + beside_back.astype(F32)
        plane = plane.astype(BF16)
        if group == (0,):
            arrived.append(plane)
        else:
            for i, shift in enumerate(group):
                piece = plane[i * tok_count : (i + 1) * tok_count]
                arrived.append(send(piece, level_route(count, levels - shift)))

    blocks = [block for group in blocks_of for block in group]
    grads = weight_grads(blocks, all_hidden, all_pairs, width, w_gate.shape[1])

    total = sum(piece.astype(F32) for piece in arrived)
    grad_tokens = total[:, :width].astype(BF16)
    gate_sums = total[:, width:]
    grad_gates = jnp.sum(jnp.where(chosen, gate_sums[:, None, :], 0.0), axis=2).astype(BF16)
    return (grad_tokens, grad_gates, *grads)


def solution(mesh):
    rows = P(("group", "expert"), None)
    return jax.shard_map(
        local,
        mesh=mesh,
        in_specs=(rows, rows, rows, rows, P("group", "expert"), P("group", "expert"), P("expert", "group")),
        out_specs=(rows, rows, P("group", "expert"), P("group", "expert"), P("expert", "group")),
        check_vma=False,
    )
```

```python
import functools

import jax
import jax.numpy as jnp
from jax import lax
from jax.experimental import pallas as pl
from jax.experimental.pallas import tpu as pltpu
from jax.sharding import PartitionSpec as P

LANES = 128
PLANE = 4
MIB = 1024 * 1024
PACK_VMEM = 56
F32 = jnp.float32
BF16 = jnp.bfloat16


def dot(left, right, left_axis, right_axis):
    return lax.dot_general(
        left, right, (((left_axis,), (right_axis,)), ((), ())), preferred_element_type=F32
    )


def split_index(index):
    return index >> 3, index >> 2 & 1, index >> 1 & 1, index & 1


def join_index(level, u, v, core):
    return ((level * 2 + u) * 2 + v) * 2 + core


def route(count, target):
    return [(index, join_index(*target(*split_index(index)))) for index in range(count)]


def core_route(count):
    return route(count, lambda level, u, v, core: (level, u, v, 1 - core))


def first_route(count):
    return route(
        count,
        lambda level, u, v, core: (level, u, 1 - v, core) if core == 0 else (level, 1 - u, v, core),
    )


def second_route(count):
    return route(
        count,
        lambda level, u, v, core: (level, 1 - u, v, core) if core == 0 else (level, u, 1 - v, core),
    )


def corner_route(count):
    return route(count, lambda level, u, v, core: (level, 1 - u, 1 - v, core))


def level_route(count, shift):
    levels = count // (2 * PLANE)
    return route(
        count,
        lambda level, u, v, core: ((level + (-shift if core else shift)) % levels, u, v, core),
    )


def send(block, pairs):
    return lax.ppermute(block, "expert", pairs)


def after(value, *earlier):
    return lax.optimization_barrier((value, *earlier))[0]


def gate_column(gates, expert):
    lane = lax.broadcasted_iota(jnp.int32, gates.shape, 1)
    return jnp.sum(jnp.where(lane == expert, gates.astype(F32), 0.0), axis=1, keepdims=True)


def terms_body(spans, arrays, width, half, expert_ref, *refs):
    held, refs = refs[:arrays], refs[arrays:]
    weights, refs = refs[:4], refs[4:]
    *parts, own_ref, kept_ref, pre_ref = refs
    pick = lambda low, high: jnp.concatenate(
        [held[i][start : start + size, low:high] for i, start, size in spans], axis=0
    )
    expert = expert_ref[0]
    rows, grads = pick(0, width), pick(width, 2 * width)
    gates = pick(2 * width, 2 * width + LANES)
    gating = gate_column(gates, expert)
    kept_ref[:, 3 * half : 3 * half + width] = rows
    kept_ref[:, 3 * half + width :] = grads
    outs = own_ref, kept_ref
    gate_grad = 0.0
    for side in range(2):
        both_w, down_w = weights[2 * side : 2 * side + 2]
        backward = dot(grads, down_w[...], 1, 1)
        pre_ref[...] = dot(rows, both_w[...], 1, 0)
        total = 0.0
        for low in range(0, half, LANES):
            span = slice(low, low + LANES)
            pre_gate = pre_ref[:, span]
            pre_up = pre_ref[:, half + low : half + low + LANES]
            back = backward[:, span]
            logistic = jax.nn.sigmoid(pre_gate)
            activated = pre_gate * logistic
            hidden = (activated * pre_up).astype(BF16)
            total = total + hidden.astype(F32) * back
            grad_hidden = gating * back
            grad_gate = grad_hidden * pre_up * logistic * (1.0 + pre_gate * (1.0 - logistic))
            grad_up = grad_hidden * activated
            out = outs[side]
            out[:, span] = grad_gate.astype(BF16)
            out[:, half + low : half + low + LANES] = grad_up.astype(BF16)
            scaled = gating * (activated * pre_up)
            out[:, 2 * half + low : 2 * half + low + LANES] = scaled.astype(BF16)
        gate_grad += jnp.sum(total, axis=1, keepdims=True).astype(BF16).astype(F32)
    lane = lax.broadcasted_iota(jnp.int32, gates.shape, 1)
    gate_lanes = jnp.where(lane == expert, gate_grad, 0.0).astype(BF16)
    scatter(gate_lanes, parts, slice(width, None))
    tile = 512 if width % 512 == 0 else width
    for low in range(0, width, tile):
        span = slice(low, low + tile)
        token = 0.0
        for both_w, out in zip(weights[::2], outs):
            token += dot(out[:, : 2 * half], both_w[span, :], 1, 1)
        scatter(token.astype(BF16), parts, span)


def scatter(value, parts, span):
    start = 0
    for part in parts:
        stop = start + part.shape[0]
        part[:, span] = value[start:stop]
        start = stop


def expert_terms(blocks, weights, expert):
    half, width = weights[1].shape
    arrays = []
    for place in blocks:
        for array, _, _ in place:
            if not any(array is known for known in arrays):
                arrays.append(array)
    number = lambda array: [array is known for known in arrays].index(True)
    spans = [(number(array), start, size) for place in blocks for array, start, size in place]
    sizes = [sum(size for _, _, size in place) for place in blocks]
    total = sum(sizes)
    whole = pl.BlockSpec(memory_space=pltpu.VMEM)
    out_shape = [jax.ShapeDtypeStruct((size, width + LANES), BF16) for size in sizes]
    out_shape.append(jax.ShapeDtypeStruct((total, 3 * half), BF16))
    out_shape.append(jax.ShapeDtypeStruct((total, 2 * width + 3 * half), BF16))
    *parts, own, kept = pl.pallas_call(
        functools.partial(terms_body, spans, len(arrays), width, half),
        out_shape=out_shape,
        in_specs=[pl.BlockSpec(memory_space=pltpu.SMEM)] + [whole] * (len(arrays) + 4),
        out_specs=[whole] * len(out_shape),
        scratch_shapes=[pltpu.VMEM((total, 2 * half), F32)],
        compiler_params=pltpu.CompilerParams(vmem_limit_bytes=16 * MIB),
        cost_estimate=pl.CostEstimate(
            flops=total * width, bytes_accessed=total * width, transcendentals=0
        ),
        name="expert_terms",
    )(expert, *arrays, *weights)
    return parts, own, kept


def stack_body(sizes, *refs):
    blocks = list(refs[: sum(sizes)])
    for size, out in zip(sizes, refs[sum(sizes) :]):
        start = 0
        for _ in range(size):
            block = blocks.pop(0)
            out[start : start + block.shape[0], :] = block[...]
            start += block.shape[0]


def stacks(*lists):
    return pl.pallas_call(
        functools.partial(stack_body, [len(blocks) for blocks in lists]),
        out_shape=[
            jax.ShapeDtypeStruct((sum(b.shape[0] for b in blocks), blocks[0].shape[1]), BF16)
            for blocks in lists
        ],
        compiler_params=pltpu.CompilerParams(vmem_limit_bytes=8 * MIB),
        name="stacks",
    )(*(block for blocks in lists for block in blocks))


def grads_body(groups, width, half, *refs):
    rows, refs = refs[:groups], refs[groups:]
    terms, refs = refs[:groups], refs[groups:]
    gate_out, up_out, down_out, held, sems = refs
    tile = gate_out.shape[0]
    step, steps = pl.program_id(0), pl.num_programs(0)

    def copies(at, slot):
        start = 0
        for i, block in enumerate(rows):
            size = block.shape[0]
            for side in range(2):
                source = pl.ds(pl.multiple_of(3 * half + side * width + at * tile, LANES), tile)
                yield pltpu.make_async_copy(
                    block.at[:, source],
                    held.at[slot, side, pl.ds(start, size), :],
                    sems.at[slot, side, i],
                )
            start += size

    @pl.when(step == 0)
    def _():
        for copy in copies(0, 0):
            copy.start()

    @pl.when(step + 1 < steps)
    def _():
        for copy in copies(step + 1, (step + 1) % 2):
            copy.start()

    slot = step % 2
    for copy in copies(step, slot):
        copy.wait()
    pairs = jnp.concatenate([term[:, : 2 * half] for term in terms], axis=0)
    hidden = jnp.concatenate([term[:, 2 * half :] for term in terms], axis=0)
    both = dot(held[slot, 0], pairs, 0, 0).astype(BF16)
    gate_out[...] = both[:, :half]
    up_out[...] = both[:, half:]
    down_out[...] = dot(hidden, held[slot, 1], 0, 0).astype(BF16)


def weight_grads(rows, terms, width, half):
    groups = len(rows)
    total = sum(block.shape[0] for block in rows)
    tile = width // 2 if total <= 1024 else width // 8
    column = pl.BlockSpec((tile, half), lambda i: (i, 0))
    return pl.pallas_call(
        functools.partial(grads_body, groups, width, half),
        grid=(width // tile,),
        out_shape=[jax.ShapeDtypeStruct((width, half), BF16)] * 2
        + [jax.ShapeDtypeStruct((half, width), BF16)],
        in_specs=[pl.BlockSpec(memory_space=pl.ANY)] * groups
        + [pl.BlockSpec((term.shape[0], 3 * half), lambda i: (0, 0)) for term in terms],
        out_specs=[column, column, pl.BlockSpec((half, tile), lambda i: (0, i))],
        scratch_shapes=[
            pltpu.VMEM((2, 2, total, tile), BF16),
            pltpu.SemaphoreType.DMA((2, 2, groups)),
        ],
        compiler_params=pltpu.CompilerParams(vmem_limit_bytes=(28 if total <= 1024 else 48) * MIB),
        cost_estimate=pl.CostEstimate(
            flops=2 * 3 * total * width * half,
            bytes_accessed=4 * total * width + 6 * width * half,
            transcendentals=0,
        ),
        name="weight_grads",
    )(*rows, *terms)


def add(left, right):
    return (left.astype(F32) + right.astype(F32)).astype(BF16)


def local(tokens, upstream, expert_ids, gate_weights, w_gate, w_up, w_down):
    tok_count, width = tokens.shape
    half = w_gate.shape[1]
    count = lax.axis_size("expert")
    levels = count // (2 * PLANE)
    expert = (lax.axis_index("expert") // 2).astype(jnp.int32)[None]
    chosen = expert_ids[:, :, None] == jnp.arange(LANES, dtype=jnp.int32)[None, None, :]
    gates = jnp.sum(jnp.where(chosen, gate_weights.astype(F32)[:, :, None], 0.0), axis=1)
    home = jnp.concatenate([tokens, upstream, gates.astype(BF16)], axis=1)

    first, second, corner = first_route(count), second_route(count), corner_route(count)
    swap = core_route(count)
    onward, backward = level_route(count, 1), level_route(count, -1)
    both = jnp.concatenate([w_gate, w_up], axis=1)
    weights = [both, w_down, send(both, swap)]
    last = levels // 2

    ways = {1: (home, None), -1: (home, None)}
    units, results, planes, arrived, rows, terms = [], [], {}, [], [], []
    done = ()
    for step in range(last + 4):
        ready, done, sent = done, [], ()

        def pass_on(block, pairs):
            result = send(after(block, *ready) if ready else block, pairs)
            done.append(result)
            return result

        if step <= last:
            here = [way for way in (1, -1) if step and ways[way][0] is not None]
            lists = [[ways[way][0] for way in here]]
            for way in here:
                if step + 1 < last or (way == 1 and step < last):
                    lists.append(list(ways[way]))
            lists = [blocks for blocks in lists if len(blocks) > 1]
            stacked = list(stacks(*lists)) if lists else []
            mine = home if step == 0 else stacked.pop(0) if len(here) > 1 else ways[1][0]
            new, corners = {1: (None, None), -1: (None, None)}, []
            for way in (1, -1):
                goes_on = step < last if way == 1 else step + 1 < last
                pairs = level_route(count, way)
                if step == 0:
                    if goes_on:
                        new[way] = (pass_on(home, pairs), None)
                elif way in here:
                    got = pass_on(stacked.pop(0) if goes_on else ways[way][1], pairs)
                    corner_at = tok_count if goes_on else 0
                    corners.append((got, corner_at, tok_count))
                    if goes_on:
                        new[way] = (got[:tok_count], got[tok_count:])
                    else:
                        new[way] = (None, got)
            sent = (mine,)
            near, beside = pass_on(mine, first), pass_on(mine, second)
            if step == 0:
                across = send(beside, first)
                done.append(across)
                corners = [(across, 0, tok_count)]
                new = {way: (new[way][0], across) for way in new}
            if step == 1:
                weights.append(send(after(w_down, *ready), swap))
            units.append([[(block, 0, block.shape[0])] for block in (mine, near, beside)] + [corners])
            ways = new
        if 1 <= step - 2 <= last:
            at = step - 3
            beside_back = pass_on(add(results[at][2], across_back), second)
            planes[at] = [results[at][0], near_back, beside_back]
        if 0 <= step - 2 <= last:
            at = step - 2
            if at < last:
                across_back, near_back = pass_on(results[at][3], first), pass_on(results[at][1], first)
            else:
                pieces = [pass_on(part, pairs) for part, pairs in zip(results[at][1:], (first, second, corner))]
                planes[at] = [results[at][0], *pieces]
            pass_on(rows[2 * at], swap)
            rows[2 * at + 1] = terms[2 * at + 1] = done[-1]
        if 0 <= step - 1 <= last:
            unit = units[step - 1]
            block, *span = unit[0][0]
            unit[0][0] = (after(block, *ready, *sent), *span)
            parts, own, kept = expert_terms(unit, weights, expert)
            done.append(parts[0])
            results.append(parts)
            rows += [kept, None]
            terms += [own, None]
        back_home = [at for at in planes if planes[at] and (at < last - 1 or step == last + 3)]
        if step >= 3:
            for at in back_home:
                plane = sum(piece.astype(F32) for piece in planes[at]).astype(BF16)
                planes[at] = None
                if at == 0:
                    arrived.append(plane)
                else:
                    arrived.append(pass_on(plane[:tok_count], level_route(count, -at)))
                if plane.shape[0] > tok_count:
                    arrived.append(pass_on(plane[tok_count:], level_route(count, at)))

    grads = weight_grads(rows, terms, width, half)
    arrived[-1] = after(arrived[-1], *grads)

    grad_tokens = sum(piece[:, :width].astype(F32) for piece in arrived).astype(BF16)
    gate_sums = sum(piece[:, width:].astype(F32) for piece in arrived)
    grad_gates = jnp.sum(jnp.where(chosen, gate_sums[:, None, :], 0.0), axis=2).astype(BF16)
    return (grad_tokens, grad_gates, *grads)


def solution(mesh):
    rows = P(("group", "expert"), None)
    return jax.shard_map(
        local,
        mesh=mesh,
        in_specs=(rows, rows, rows, rows, P("group", "expert"), P("group", "expert"), P("expert", "group")),
        out_specs=(rows, rows, P("group", "expert"), P("group", "expert"), P("expert", "group")),
        check_vma=False,
    )
```

```python
import functools

import jax
import jax.numpy as jnp
from jax import lax
from jax.experimental import pallas as pl
from jax.experimental.pallas import tpu as pltpu
from jax.sharding import PartitionSpec as P

LANES = 128
PLANE = 4
MIB = 1024 * 1024
PACK_VMEM = 56
F32 = jnp.float32
BF16 = jnp.bfloat16


def dot(left, right, left_axis, right_axis):
    return lax.dot_general(
        left, right, (((left_axis,), (right_axis,)), ((), ())), preferred_element_type=F32
    )


def split_index(index):
    return index >> 3, index >> 2 & 1, index >> 1 & 1, index & 1


def join_index(level, u, v, core):
    return ((level * 2 + u) * 2 + v) * 2 + core


def route(count, target):
    return [(index, join_index(*target(*split_index(index)))) for index in range(count)]


def core_route(count):
    return route(count, lambda level, u, v, core: (level, u, v, 1 - core))


def first_route(count):
    return route(
        count,
        lambda level, u, v, core: (level, u, 1 - v, core) if core == 0 else (level, 1 - u, v, core),
    )


def second_route(count):
    return route(
        count,
        lambda level, u, v, core: (level, 1 - u, v, core) if core == 0 else (level, u, 1 - v, core),
    )


def corner_route(count):
    return route(count, lambda level, u, v, core: (level, 1 - u, 1 - v, core))


def level_route(count, shift):
    levels = count // (2 * PLANE)
    return route(
        count,
        lambda level, u, v, core: ((level + (-shift if core else shift)) % levels, u, v, core),
    )


def send(block, pairs):
    return lax.ppermute(block, "expert", pairs)


def after(value, *earlier):
    return lax.optimization_barrier((value, *earlier))[0]


def gate_column(gates, expert):
    lane = lax.broadcasted_iota(jnp.int32, gates.shape, 1)
    return jnp.sum(jnp.where(lane == expert, gates.astype(F32), 0.0), axis=1, keepdims=True)


def terms_body(spans, arrays, width, half, expert_ref, *refs):
    held, refs = refs[:arrays], refs[arrays:]
    weights, refs = refs[:4], refs[4:]
    *parts, own_ref, kept_ref, pre_ref = refs
    pick = lambda low, high: jnp.concatenate(
        [held[i][start : start + size, low:high] for i, start, size in spans], axis=0
    )
    expert = expert_ref[0]
    rows, grads = pick(0, width), pick(width, 2 * width)
    gates = pick(2 * width, 2 * width + LANES)
    gating = gate_column(gates, expert)
    kept_ref[:, 3 * half : 3 * half + width] = rows
    kept_ref[:, 3 * half + width :] = grads
    outs = own_ref, kept_ref
    gate_grad = 0.0
    for side in range(2):
        both_w, down_w = weights[2 * side : 2 * side + 2]
        backward = dot(grads, down_w[...], 1, 1)
        pre_ref[...] = dot(rows, both_w[...], 1, 0)
        total = 0.0
        for low in range(0, half, LANES):
            span = slice(low, low + LANES)
            pre_gate = pre_ref[:, span]
            pre_up = pre_ref[:, half + low : half + low + LANES]
            back = backward[:, span]
            logistic = jax.nn.sigmoid(pre_gate)
            activated = pre_gate * logistic
            hidden = (activated * pre_up).astype(BF16)
            total = total + hidden.astype(F32) * back
            grad_hidden = gating * back
            grad_gate = grad_hidden * pre_up * logistic * (1.0 + pre_gate * (1.0 - logistic))
            grad_up = grad_hidden * activated
            out = outs[side]
            out[:, span] = grad_gate.astype(BF16)
            out[:, half + low : half + low + LANES] = grad_up.astype(BF16)
            scaled = gating * (activated * pre_up)
            out[:, 2 * half + low : 2 * half + low + LANES] = scaled.astype(BF16)
        gate_grad += jnp.sum(total, axis=1, keepdims=True).astype(BF16).astype(F32)
    lane = lax.broadcasted_iota(jnp.int32, gates.shape, 1)
    gate_lanes = jnp.where(lane == expert, gate_grad, 0.0).astype(BF16)
    scatter(gate_lanes, parts, slice(width, None))
    tile = 512 if width % 512 == 0 else width
    for low in range(0, width, tile):
        span = slice(low, low + tile)
        token = 0.0
        for both_w, out in zip(weights[::2], outs):
            token += dot(out[:, : 2 * half], both_w[span, :], 1, 1)
        scatter(token.astype(BF16), parts, span)


def scatter(value, parts, span):
    start = 0
    for part in parts:
        stop = start + part.shape[0]
        part[:, span] = value[start:stop]
        start = stop


def expert_terms(blocks, weights, expert):
    half, width = weights[1].shape
    arrays = []
    for place in blocks:
        for array, _, _ in place:
            if not any(array is known for known in arrays):
                arrays.append(array)
    number = lambda array: [array is known for known in arrays].index(True)
    spans = [(number(array), start, size) for place in blocks for array, start, size in place]
    sizes = [sum(size for _, _, size in place) for place in blocks]
    total = sum(sizes)
    whole = pl.BlockSpec(memory_space=pltpu.VMEM)
    out_shape = [jax.ShapeDtypeStruct((size, width + LANES), BF16) for size in sizes]
    out_shape.append(jax.ShapeDtypeStruct((total, 3 * half), BF16))
    out_shape.append(jax.ShapeDtypeStruct((total, 2 * width + 3 * half), BF16))
    *parts, own, kept = pl.pallas_call(
        functools.partial(terms_body, spans, len(arrays), width, half),
        out_shape=out_shape,
        in_specs=[pl.BlockSpec(memory_space=pltpu.SMEM)] + [whole] * (len(arrays) + 4),
        out_specs=[whole] * len(out_shape),
        scratch_shapes=[pltpu.VMEM((total, 2 * half), F32)],
        compiler_params=pltpu.CompilerParams(vmem_limit_bytes=10 * MIB),
        cost_estimate=pl.CostEstimate(
            flops=total * width, bytes_accessed=total * width, transcendentals=0
        ),
        name="expert_terms",
    )(expert, *arrays, *weights)
    return parts, own, kept


def stack_body(sizes, *refs):
    blocks = list(refs[: sum(sizes)])
    for size, out in zip(sizes, refs[sum(sizes) :]):
        start = 0
        for _ in range(size):
            block = blocks.pop(0)
            out[start : start + block.shape[0], :] = block[...]
            start += block.shape[0]


def stacks(*lists):
    return pl.pallas_call(
        functools.partial(stack_body, [len(blocks) for blocks in lists]),
        out_shape=[
            jax.ShapeDtypeStruct((sum(b.shape[0] for b in blocks), blocks[0].shape[1]), BF16)
            for blocks in lists
        ],
        compiler_params=pltpu.CompilerParams(vmem_limit_bytes=8 * MIB),
        name="stacks",
    )(*(block for blocks in lists for block in blocks))


def grads_body(groups, width, half, *refs):
    rows, refs = refs[:groups], refs[groups:]
    terms, refs = refs[:groups], refs[groups:]
    gate_out, up_out, down_out, held, sems = refs
    tile = gate_out.shape[0]
    step, steps = pl.program_id(0), pl.num_programs(0)

    def copies(at, slot):
        start = 0
        for i, block in enumerate(rows):
            size = block.shape[0]
            for side in range(2):
                source = pl.ds(pl.multiple_of(3 * half + side * width + at * tile, LANES), tile)
                yield pltpu.make_async_copy(
                    block.at[:, source],
                    held.at[slot, side, pl.ds(start, size), :],
                    sems.at[slot, side, i],
                )
            start += size

    @pl.when(step == 0)
    def _():
        for copy in copies(0, 0):
            copy.start()

    @pl.when(step + 1 < steps)
    def _():
        for copy in copies(step + 1, (step + 1) % 2):
            copy.start()

    slot = step % 2
    for copy in copies(step, slot):
        copy.wait()
    pairs = jnp.concatenate([term[:, : 2 * half] for term in terms], axis=0)
    hidden = jnp.concatenate([term[:, 2 * half :] for term in terms], axis=0)
    both = dot(held[slot, 0], pairs, 0, 0).astype(BF16)
    gate_out[...] = both[:, :half]
    up_out[...] = both[:, half:]
    down_out[...] = dot(hidden, held[slot, 1], 0, 0).astype(BF16)


def weight_grads(rows, terms, width, half):
    groups = len(rows)
    total = sum(block.shape[0] for block in rows)
    tile = width // 2 if total <= 1024 else width // 8
    column = pl.BlockSpec((tile, half), lambda i: (i, 0))
    return pl.pallas_call(
        functools.partial(grads_body, groups, width, half),
        grid=(width // tile,),
        out_shape=[jax.ShapeDtypeStruct((width, half), BF16)] * 2
        + [jax.ShapeDtypeStruct((half, width), BF16)],
        in_specs=[pl.BlockSpec(memory_space=pl.ANY)] * groups
        + [pl.BlockSpec((term.shape[0], 3 * half), lambda i: (0, 0)) for term in terms],
        out_specs=[column, column, pl.BlockSpec((half, tile), lambda i: (0, i))],
        scratch_shapes=[
            pltpu.VMEM((2, 2, total, tile), BF16),
            pltpu.SemaphoreType.DMA((2, 2, groups)),
        ],
        compiler_params=pltpu.CompilerParams(vmem_limit_bytes=(22 if total <= 1024 else 48) * MIB),
        cost_estimate=pl.CostEstimate(
            flops=2 * 3 * total * width * half,
            bytes_accessed=4 * total * width + 6 * width * half,
            transcendentals=0,
        ),
        name="weight_grads",
    )(*rows, *terms)


def add(left, right):
    return (left.astype(F32) + right.astype(F32)).astype(BF16)


def local(tokens, upstream, expert_ids, gate_weights, w_gate, w_up, w_down):
    tok_count, width = tokens.shape
    half = w_gate.shape[1]
    count = lax.axis_size("expert")
    levels = count // (2 * PLANE)
    expert = (lax.axis_index("expert") // 2).astype(jnp.int32)[None]
    chosen = expert_ids[:, :, None] == jnp.arange(LANES, dtype=jnp.int32)[None, None, :]
    gates = jnp.sum(jnp.where(chosen, gate_weights.astype(F32)[:, :, None], 0.0), axis=1)
    home = jnp.concatenate([tokens, upstream, gates.astype(BF16)], axis=1)

    first, second, corner = first_route(count), second_route(count), corner_route(count)
    swap = core_route(count)
    onward, backward = level_route(count, 1), level_route(count, -1)
    both = jnp.concatenate([w_gate, w_up], axis=1)
    weights = [both, w_down, send(both, swap)]
    weights.append(send(w_down, swap))
    last = levels // 2
    groups = [(at, -at) if 0 < 2 * at < levels else (at,) for at in range(last + 1)]

    ways = {1: (home, None), -1: (home, None)}
    units, results, planes, arrived, far, rows, terms = [], [], {}, [], [], [], []
    done = ()
    for step in range(last + 4):
        ready, done, sent = done, [], ()

        def pass_on(block, pairs):
            result = send(after(block, *ready) if ready else block, pairs)
            done.append(result)
            return result

        if step <= last:
            here = [way for way in (1, -1) if step and ways[way][0] is not None]
            lists = [[ways[way][0] for way in here]]
            for way in here:
                if step + 1 < last or (way == 1 and step < last):
                    lists.append(list(ways[way]))
            lists = [blocks for blocks in lists if len(blocks) > 1]
            stacked = list(stacks(*lists)) if lists else []
            mine = home if step == 0 else stacked.pop(0) if len(here) > 1 else ways[1][0]
            new, corners = {1: (None, None), -1: (None, None)}, []
            for way in (1, -1):
                goes_on = step < last if way == 1 else step + 1 < last
                pairs = level_route(count, way)
                if step == 0:
                    if goes_on:
                        new[way] = (pass_on(home, pairs), None)
                elif way in here:
                    got = pass_on(stacked.pop(0) if goes_on else ways[way][1], pairs)
                    corner_at = tok_count if goes_on else 0
                    corners.append((got, corner_at, tok_count))
                    if goes_on:
                        new[way] = (got[:tok_count], got[tok_count:])
                    else:
                        new[way] = (None, got)
            sent = (mine,)
            beside = pass_on(mine, second)
            near = pass_on(mine if step else after(home, beside, *weights[2:]), first)
            if step == 0:
                across = send(beside, first)
                done.append(across)
                corners = [(across, 0, tok_count)]
                new = {way: (new[way][0], across) for way in new}
            own_blocks = [(ways[way][0], 0, tok_count) for way in here] or [(home, 0, tok_count)]
            units.append([own_blocks] + [[(block, 0, block.shape[0])] for block in (near, beside)] + [corners])
            ways = new
        if 1 <= step - 3 <= last:
            at = step - 3
            plane = sum(part.astype(F32) for part in planes[at]).astype(BF16)
            for i, shift in enumerate(groups[at]):
                piece = plane[i * tok_count : (i + 1) * tok_count]
                arrived.append(pass_on(piece, level_route(count, -shift)))
        if 0 <= step - 2 <= last:
            at = step - 2
            parts = results[at]
            planes[at] = [parts[0], pass_on(parts[1], first)]
            if at:
                planes[at].append(pass_on(parts[2], second))
            if at == last:
                planes[at].append(pass_on(parts[3], corner))
            elif at:
                for i, shift in enumerate(groups[at]):
                    piece = parts[3][i * tok_count : (i + 1) * tok_count]
                    far.append(pass_on(piece, level_route(count, -shift)))
        if step == last + 3:
            relayed = pass_on(sum(part.astype(F32) for part in (results[0][3], *far)).astype(BF16), first)
            arrived += [*planes[0], send(add(results[0][2], relayed), second)]
        if 3 <= step:
            rows[2 * step - 5] = terms[2 * step - 5] = send(rows[2 * step - 6], swap)
        if 0 <= step - 1 <= last:
            unit = units[step - 1]
            block, *span = unit[0][0]
            unit[0][0] = (after(block, *ready, *sent), *span)
            parts, own, kept = expert_terms(unit, weights, expert)
            done.append(parts[0])
            results.append(parts)
            rows += [kept, None]
            terms += [own, None]

    grads = weight_grads(rows, terms, width, half)
    arrived[-1] = after(arrived[-1], *grads)

    grad_tokens = sum(piece[:, :width].astype(F32) for piece in arrived).astype(BF16)
    gate_sums = sum(piece[:, width:].astype(F32) for piece in arrived)
    grad_gates = jnp.sum(jnp.where(chosen, gate_sums[:, None, :], 0.0), axis=2).astype(BF16)
    return (grad_tokens, grad_gates, *grads)


def solution(mesh):
    rows = P(("group", "expert"), None)
    return jax.shard_map(
        local,
        mesh=mesh,
        in_specs=(rows, rows, rows, rows, P("group", "expert"), P("group", "expert"), P("expert", "group")),
        out_specs=(rows, rows, P("group", "expert"), P("group", "expert"), P("expert", "group")),
        check_vma=False,
    )
```

```python
import functools

import jax
import jax.numpy as jnp
from jax import lax
from jax.experimental import pallas as pl
from jax.experimental.pallas import tpu as pltpu
from jax.sharding import PartitionSpec as P

LANES = 128
PLANE = 4
MIB = 1024 * 1024
PACK_VMEM = 56
F32 = jnp.float32
BF16 = jnp.bfloat16


def dot(left, right, left_axis, right_axis):
    return lax.dot_general(
        left, right, (((left_axis,), (right_axis,)), ((), ())), preferred_element_type=F32
    )


def split_index(index):
    return index >> 3, index >> 2 & 1, index >> 1 & 1, index & 1


def join_index(level, u, v, core):
    return ((level * 2 + u) * 2 + v) * 2 + core


def route(count, target):
    return [(index, join_index(*target(*split_index(index)))) for index in range(count)]


def core_route(count):
    return route(count, lambda level, u, v, core: (level, u, v, 1 - core))


def first_route(count):
    return route(
        count,
        lambda level, u, v, core: (level, u, 1 - v, core) if core == 0 else (level, 1 - u, v, core),
    )


def second_route(count):
    return route(
        count,
        lambda level, u, v, core: (level, 1 - u, v, core) if core == 0 else (level, u, 1 - v, core),
    )


def corner_route(count):
    return route(count, lambda level, u, v, core: (level, 1 - u, 1 - v, core))


def level_route(count, shift):
    levels = count // (2 * PLANE)
    return route(
        count,
        lambda level, u, v, core: ((level + (-shift if core else shift)) % levels, u, v, core),
    )


def send(block, pairs):
    return lax.ppermute(block, "expert", pairs)


def after(value, *earlier):
    return lax.optimization_barrier((value, *earlier))[0]


def gate_column(gates, expert):
    lane = lax.broadcasted_iota(jnp.int32, gates.shape, 1)
    return jnp.sum(jnp.where(lane == expert, gates.astype(F32), 0.0), axis=1, keepdims=True)


def terms_body(spans, arrays, width, half, expert_ref, *refs):
    held, refs = refs[:arrays], refs[arrays:]
    weights, refs = refs[:4], refs[4:]
    *parts, own_ref, kept_ref, pre_ref = refs
    pick = lambda low, high: jnp.concatenate(
        [held[i][start : start + size, low:high] for i, start, size in spans], axis=0
    )
    expert = expert_ref[0]
    rows, grads = pick(0, width), pick(width, 2 * width)
    gates = pick(2 * width, 2 * width + LANES)
    gating = gate_column(gates, expert)
    kept_ref[:, 3 * half : 3 * half + width] = rows
    kept_ref[:, 3 * half + width :] = grads
    outs = own_ref, kept_ref
    gate_grad = 0.0
    for side in range(2):
        both_w, down_w = weights[2 * side : 2 * side + 2]
        backward = dot(grads, down_w[...], 1, 1)
        pre_ref[...] = dot(rows, both_w[...], 1, 0)
        total = 0.0
        for low in range(0, half, LANES):
            span = slice(low, low + LANES)
            pre_gate = pre_ref[:, span]
            pre_up = pre_ref[:, half + low : half + low + LANES]
            back = backward[:, span]
            logistic = jax.nn.sigmoid(pre_gate)
            activated = pre_gate * logistic
            hidden = (activated * pre_up).astype(BF16)
            total = total + hidden.astype(F32) * back
            grad_hidden = gating * back
            grad_gate = grad_hidden * pre_up * logistic * (1.0 + pre_gate * (1.0 - logistic))
            grad_up = grad_hidden * activated
            out = outs[side]
            out[:, span] = grad_gate.astype(BF16)
            out[:, half + low : half + low + LANES] = grad_up.astype(BF16)
            scaled = gating * (activated * pre_up)
            out[:, 2 * half + low : 2 * half + low + LANES] = scaled.astype(BF16)
        gate_grad += jnp.sum(total, axis=1, keepdims=True).astype(BF16).astype(F32)
    lane = lax.broadcasted_iota(jnp.int32, gates.shape, 1)
    gate_lanes = jnp.where(lane == expert, gate_grad, 0.0).astype(BF16)
    scatter(gate_lanes, parts, slice(width, None))
    tile = 512 if width % 512 == 0 else width
    for low in range(0, width, tile):
        span = slice(low, low + tile)
        token = 0.0
        for both_w, out in zip(weights[::2], outs):
            token += dot(out[:, : 2 * half], both_w[span, :], 1, 1)
        scatter(token.astype(BF16), parts, span)


def scatter(value, parts, span):
    start = 0
    for part in parts:
        stop = start + part.shape[0]
        part[:, span] = value[start:stop]
        start = stop


def expert_terms(blocks, weights, expert):
    half, width = weights[1].shape
    arrays = []
    for place in blocks:
        for array, _, _ in place:
            if not any(array is known for known in arrays):
                arrays.append(array)
    number = lambda array: [array is known for known in arrays].index(True)
    spans = [(number(array), start, size) for place in blocks for array, start, size in place]
    sizes = [sum(size for _, _, size in place) for place in blocks]
    total = sum(sizes)
    whole = pl.BlockSpec(memory_space=pltpu.VMEM)
    out_shape = [jax.ShapeDtypeStruct((size, width + LANES), BF16) for size in sizes]
    out_shape.append(jax.ShapeDtypeStruct((total, 3 * half), BF16))
    out_shape.append(jax.ShapeDtypeStruct((total, 2 * width + 3 * half), BF16))
    *parts, own, kept = pl.pallas_call(
        functools.partial(terms_body, spans, len(arrays), width, half),
        out_shape=out_shape,
        in_specs=[pl.BlockSpec(memory_space=pltpu.SMEM)] + [whole] * (len(arrays) + 4),
        out_specs=[whole] * len(out_shape),
        scratch_shapes=[pltpu.VMEM((total, 2 * half), F32)],
        compiler_params=pltpu.CompilerParams(vmem_limit_bytes=10 * MIB),
        cost_estimate=pl.CostEstimate(
            flops=total * width, bytes_accessed=total * width, transcendentals=0
        ),
        name="expert_terms",
    )(expert, *arrays, *weights)
    return parts, own, kept


def stack_body(sizes, *refs):
    blocks = list(refs[: sum(sizes)])
    for size, out in zip(sizes, refs[sum(sizes) :]):
        start = 0
        for _ in range(size):
            block = blocks.pop(0)
            out[start : start + block.shape[0], :] = block[...]
            start += block.shape[0]


def stacks(*lists):
    return pl.pallas_call(
        functools.partial(stack_body, [len(blocks) for blocks in lists]),
        out_shape=[
            jax.ShapeDtypeStruct((sum(b.shape[0] for b in blocks), blocks[0].shape[1]), BF16)
            for blocks in lists
        ],
        compiler_params=pltpu.CompilerParams(vmem_limit_bytes=8 * MIB),
        name="stacks",
    )(*(block for blocks in lists for block in blocks))


def grads_body(groups, width, half, *refs):
    rows, refs = refs[:groups], refs[groups:]
    terms, refs = refs[:groups], refs[groups:]
    gate_out, up_out, down_out, held, sems = refs
    tile = gate_out.shape[0]
    step, steps = pl.program_id(0), pl.num_programs(0)

    def copies(at, slot):
        start = 0
        for i, block in enumerate(rows):
            size = block.shape[0]
            for side in range(2):
                source = pl.ds(pl.multiple_of(3 * half + side * width + at * tile, LANES), tile)
                yield pltpu.make_async_copy(
                    block.at[:, source],
                    held.at[slot, side, pl.ds(start, size), :],
                    sems.at[slot, side, i],
                )
            start += size

    @pl.when(step == 0)
    def _():
        for copy in copies(0, 0):
            copy.start()

    @pl.when(step + 1 < steps)
    def _():
        for copy in copies(step + 1, (step + 1) % 2):
            copy.start()

    slot = step % 2
    for copy in copies(step, slot):
        copy.wait()
    pairs = jnp.concatenate([term[:, : 2 * half] for term in terms], axis=0)
    hidden = jnp.concatenate([term[:, 2 * half :] for term in terms], axis=0)
    both = dot(held[slot, 0], pairs, 0, 0).astype(BF16)
    gate_out[...] = both[:, :half]
    up_out[...] = both[:, half:]
    down_out[...] = dot(hidden, held[slot, 1], 0, 0).astype(BF16)


def weight_grads(rows, terms, width, half):
    groups = len(rows)
    total = sum(block.shape[0] for block in rows)
    tile = width // 2 if total <= 1024 else width // 8
    column = pl.BlockSpec((tile, half), lambda i: (i, 0))
    return pl.pallas_call(
        functools.partial(grads_body, groups, width, half),
        grid=(width // tile,),
        out_shape=[jax.ShapeDtypeStruct((width, half), BF16)] * 2
        + [jax.ShapeDtypeStruct((half, width), BF16)],
        in_specs=[pl.BlockSpec(memory_space=pl.ANY)] * groups
        + [pl.BlockSpec((term.shape[0], 3 * half), lambda i: (0, 0)) for term in terms],
        out_specs=[column, column, pl.BlockSpec((half, tile), lambda i: (0, i))],
        scratch_shapes=[
            pltpu.VMEM((2, 2, total, tile), BF16),
            pltpu.SemaphoreType.DMA((2, 2, groups)),
        ],
        compiler_params=pltpu.CompilerParams(vmem_limit_bytes=(22 if total <= 1024 else 48) * MIB),
        cost_estimate=pl.CostEstimate(
            flops=2 * 3 * total * width * half,
            bytes_accessed=4 * total * width + 6 * width * half,
            transcendentals=0,
        ),
        name="weight_grads",
    )(*rows, *terms)


def add(left, right):
    return (left.astype(F32) + right.astype(F32)).astype(BF16)


def local(tokens, upstream, expert_ids, gate_weights, w_gate, w_up, w_down):
    tok_count, width = tokens.shape
    half = w_gate.shape[1]
    count = lax.axis_size("expert")
    levels = count // (2 * PLANE)
    expert = (lax.axis_index("expert") // 2).astype(jnp.int32)[None]
    chosen = expert_ids[:, :, None] == jnp.arange(LANES, dtype=jnp.int32)[None, None, :]
    gates = jnp.sum(jnp.where(chosen, gate_weights.astype(F32)[:, :, None], 0.0), axis=1)
    home = jnp.concatenate([tokens, upstream, gates.astype(BF16)], axis=1)

    first, second, corner = first_route(count), second_route(count), corner_route(count)
    swap = core_route(count)
    onward, backward = level_route(count, 1), level_route(count, -1)
    both = jnp.concatenate([w_gate, w_up], axis=1)
    weights = [both, w_down, send(both, swap)]
    weights.append(send(w_down, swap))
    last = levels // 2
    groups = [(at, -at) if 0 < 2 * at < levels else (at,) for at in range(last + 1)]

    ways = {1: (home, None), -1: (home, None)}
    units, results, planes, arrived, far, rows, terms = [], [], {}, [], [], [], []
    done = ()
    for step in range(last + 4):
        ready, done, sent = done, [], ()

        def pass_on(block, pairs):
            result = send(after(block, *ready) if ready else block, pairs)
            done.append(result)
            return result

        if step <= last:
            here = [way for way in (1, -1) if step and ways[way][0] is not None]
            lists = [[ways[way][0] for way in here]]
            for way in here:
                if step + 1 < last or (way == 1 and step < last):
                    lists.append(list(ways[way]))
            lists = [blocks for blocks in lists if len(blocks) > 1]
            stacked = list(stacks(*lists)) if lists else []
            mine = home if step == 0 else stacked.pop(0) if len(here) > 1 else ways[1][0]
            new, corners = {1: (None, None), -1: (None, None)}, []
            for way in (1, -1):
                goes_on = step < last if way == 1 else step + 1 < last
                pairs = level_route(count, way)
                if step == 0:
                    if goes_on:
                        new[way] = (pass_on(home, pairs), None)
                elif way in here:
                    got = pass_on(stacked.pop(0) if goes_on else ways[way][1], pairs)
                    corner_at = tok_count if goes_on else 0
                    corners.append((got, corner_at, tok_count))
                    if goes_on:
                        new[way] = (got[:tok_count], got[tok_count:])
                    else:
                        new[way] = (None, got)
            sent = (mine,)
            beside = pass_on(mine, second)
            near = pass_on(mine if step else after(home, beside, *weights[2:]), first)
            if step == 0:
                across = send(beside, first)
                done.append(across)
                corners = [(across, 0, tok_count)]
                new = {way: (new[way][0], across) for way in new}
            own_blocks = [(ways[way][0], 0, tok_count) for way in here] or [(home, 0, tok_count)]
            units.append([own_blocks] + [[(block, 0, block.shape[0])] for block in (near, beside)] + [corners])
            ways = new
        if 1 <= step - 3 <= last:
            at = step - 3
            plane = sum(part.astype(F32) for part in planes[at]).astype(BF16)
            for i, shift in enumerate(groups[at]):
                piece = plane[i * tok_count : (i + 1) * tok_count]
                arrived.append(pass_on(piece, level_route(count, -shift)))
        if 0 <= step - 2 <= last:
            at = step - 2
            parts = results[at]
            planes[at] = [parts[0]]
            if at:
                planes[at].append(pass_on(parts[1], first))
                planes[at].append(pass_on(parts[2], second))
            if at == last:
                planes[at].append(pass_on(parts[3], corner))
            elif at:
                for i, shift in enumerate(groups[at]):
                    piece = parts[3][i * tok_count : (i + 1) * tok_count]
                    far.append(pass_on(piece, level_route(count, -shift)))
        if step == last + 3:
            far = sum(part.astype(F32) for part in (results[0][3], *far)).astype(BF16)
            arrived += [*planes[0], pass_on(results[0][1], first), pass_on(results[0][2], second), pass_on(far, corner)]
        if last + 1 < step:
            for at in range(last + 1) if step == last + 3 else ():
                block = rows[2 * at]
                if at in (0, last):
                    block = after(block, *planes[last][1:2])
                rows[2 * at + 1] = terms[2 * at + 1] = send(block, swap)
        if 0 <= step - 1 <= last:
            unit = units[step - 1]
            block, *span = unit[0][0]
            unit[0][0] = (after(block, *ready, *sent), *span)
            parts, own, kept = expert_terms(unit, weights, expert)
            done.append(parts[0])
            results.append(parts)
            rows += [kept, None]
            terms += [own, None]

    grads = weight_grads(rows, terms, width, half)
    arrived[-1] = after(arrived[-1], *grads)

    grad_tokens = sum(piece[:, :width].astype(F32) for piece in arrived).astype(BF16)
    gate_sums = sum(piece[:, width:].astype(F32) for piece in arrived)
    grad_gates = jnp.sum(jnp.where(chosen, gate_sums[:, None, :], 0.0), axis=2).astype(BF16)
    return (grad_tokens, grad_gates, *grads)


def solution(mesh):
    rows = P(("group", "expert"), None)
    return jax.shard_map(
        local,
        mesh=mesh,
        in_specs=(rows, rows, rows, rows, P("group", "expert"), P("group", "expert"), P("expert", "group")),
        out_specs=(rows, rows, P("group", "expert"), P("group", "expert"), P("expert", "group")),
        check_vma=False,
    )
```

```python
import functools

import jax
import jax.numpy as jnp
from jax import lax
from jax.experimental import pallas as pl
from jax.experimental.pallas import tpu as pltpu
from jax.sharding import PartitionSpec as P

LANES = 128
PLANE = 4
MIB = 1024 * 1024
PACK_VMEM = 56
F32 = jnp.float32
BF16 = jnp.bfloat16


def dot(left, right, left_axis, right_axis):
    return lax.dot_general(
        left, right, (((left_axis,), (right_axis,)), ((), ())), preferred_element_type=F32
    )


def split_index(index):
    return index >> 3, index >> 2 & 1, index >> 1 & 1, index & 1


def join_index(level, u, v, core):
    return ((level * 2 + u) * 2 + v) * 2 + core


def route(count, target):
    return [(index, join_index(*target(*split_index(index)))) for index in range(count)]


def core_route(count):
    return route(count, lambda level, u, v, core: (level, u, v, 1 - core))


def first_route(count):
    return route(
        count,
        lambda level, u, v, core: (level, u, 1 - v, core) if core == 0 else (level, 1 - u, v, core),
    )


def second_route(count):
    return route(
        count,
        lambda level, u, v, core: (level, 1 - u, v, core) if core == 0 else (level, u, 1 - v, core),
    )


def corner_route(count):
    return route(count, lambda level, u, v, core: (level, 1 - u, 1 - v, core))


def level_route(count, shift):
    levels = count // (2 * PLANE)
    return route(
        count,
        lambda level, u, v, core: ((level + (-shift if core else shift)) % levels, u, v, core),
    )


def send(block, pairs):
    return lax.ppermute(block, "expert", pairs)


def after(value, *earlier):
    return lax.optimization_barrier((value, *earlier))[0]


def gate_column(gates, expert):
    lane = lax.broadcasted_iota(jnp.int32, gates.shape, 1)
    return jnp.sum(jnp.where(lane == expert, gates.astype(F32), 0.0), axis=1, keepdims=True)


def terms_body(spans, arrays, width, half, expert_ref, *refs):
    held, refs = refs[:arrays], refs[arrays:]
    weights, refs = refs[:4], refs[4:]
    *parts, own_ref, kept_ref, pre_ref = refs
    pick = lambda low, high: jnp.concatenate(
        [held[i][start : start + size, low:high] for i, start, size in spans], axis=0
    )
    expert = expert_ref[0]
    rows, grads = pick(0, width), pick(width, 2 * width)
    gates = pick(2 * width, 2 * width + LANES)
    gating = gate_column(gates, expert)
    kept_ref[:, 3 * half : 3 * half + width] = rows
    kept_ref[:, 3 * half + width :] = grads
    outs = own_ref, kept_ref
    gate_grad = 0.0
    for side in range(2):
        both_w, down_w = weights[2 * side : 2 * side + 2]
        backward = dot(grads, down_w[...], 1, 1)
        pre_ref[...] = dot(rows, both_w[...], 1, 0)
        total = 0.0
        for low in range(0, half, LANES):
            span = slice(low, low + LANES)
            pre_gate = pre_ref[:, span]
            pre_up = pre_ref[:, half + low : half + low + LANES]
            back = backward[:, span]
            logistic = jax.nn.sigmoid(pre_gate)
            activated = pre_gate * logistic
            hidden = (activated * pre_up).astype(BF16)
            total = total + hidden.astype(F32) * back
            grad_hidden = gating * back
            grad_gate = grad_hidden * pre_up * logistic * (1.0 + pre_gate * (1.0 - logistic))
            grad_up = grad_hidden * activated
            out = outs[side]
            out[:, span] = grad_gate.astype(BF16)
            out[:, half + low : half + low + LANES] = grad_up.astype(BF16)
            scaled = gating * (activated * pre_up)
            out[:, 2 * half + low : 2 * half + low + LANES] = scaled.astype(BF16)
        gate_grad += jnp.sum(total, axis=1, keepdims=True).astype(BF16).astype(F32)
    lane = lax.broadcasted_iota(jnp.int32, gates.shape, 1)
    gate_lanes = jnp.where(lane == expert, gate_grad, 0.0).astype(BF16)
    scatter(gate_lanes, parts, slice(width, None))
    tile = 1024 if width % 1024 == 0 else width
    for low in range(0, width, tile):
        span = slice(low, low + tile)
        token = 0.0
        for both_w, out in zip(weights[::2], outs):
            token += dot(out[:, : 2 * half], both_w[span, :], 1, 1)
        scatter(token.astype(BF16), parts, span)


def scatter(value, parts, span):
    start = 0
    for part in parts:
        stop = start + part.shape[0]
        part[:, span] = value[start:stop]
        start = stop


def expert_terms(blocks, weights, expert):
    half, width = weights[1].shape
    arrays = []
    for place in blocks:
        for array, _, _ in place:
            if not any(array is known for known in arrays):
                arrays.append(array)
    number = lambda array: [array is known for known in arrays].index(True)
    spans = [(number(array), start, size) for place in blocks for array, start, size in place]
    sizes = [sum(size for _, _, size in place) for place in blocks]
    total = sum(sizes)
    whole = pl.BlockSpec(memory_space=pltpu.VMEM)
    out_shape = [jax.ShapeDtypeStruct((size, width + LANES), BF16) for size in sizes]
    out_shape.append(jax.ShapeDtypeStruct((total, 3 * half), BF16))
    out_shape.append(jax.ShapeDtypeStruct((total, 2 * width + 3 * half), BF16))
    *parts, own, kept = pl.pallas_call(
        functools.partial(terms_body, spans, len(arrays), width, half),
        out_shape=out_shape,
        in_specs=[pl.BlockSpec(memory_space=pltpu.SMEM)] + [whole] * (len(arrays) + 4),
        out_specs=[whole] * len(out_shape),
        scratch_shapes=[pltpu.VMEM((total, 2 * half), F32)],
        compiler_params=pltpu.CompilerParams(vmem_limit_bytes=10 * MIB),
        cost_estimate=pl.CostEstimate(
            flops=total * width, bytes_accessed=total * width, transcendentals=0
        ),
        name="expert_terms",
    )(expert, *arrays, *weights)
    return parts, own, kept


def stack_body(sizes, *refs):
    blocks = list(refs[: sum(sizes)])
    for size, out in zip(sizes, refs[sum(sizes) :]):
        start = 0
        for _ in range(size):
            block = blocks.pop(0)
            out[start : start + block.shape[0], :] = block[...]
            start += block.shape[0]


def stacks(*lists):
    return pl.pallas_call(
        functools.partial(stack_body, [len(blocks) for blocks in lists]),
        out_shape=[
            jax.ShapeDtypeStruct((sum(b.shape[0] for b in blocks), blocks[0].shape[1]), BF16)
            for blocks in lists
        ],
        compiler_params=pltpu.CompilerParams(vmem_limit_bytes=8 * MIB),
        name="stacks",
    )(*(block for blocks in lists for block in blocks))


def grads_body(groups, width, half, *refs):
    rows, refs = refs[:groups], refs[groups:]
    terms, refs = refs[:groups], refs[groups:]
    gate_out, up_out, down_out, held, sems = refs
    tile = gate_out.shape[0]
    step, steps = pl.program_id(0), pl.num_programs(0)

    def copies(at, slot):
        start = 0
        for i, block in enumerate(rows):
            size = block.shape[0]
            for side in range(2):
                source = pl.ds(pl.multiple_of(3 * half + side * width + at * tile, LANES), tile)
                yield pltpu.make_async_copy(
                    block.at[:, source],
                    held.at[slot, side, pl.ds(start, size), :],
                    sems.at[slot, side, i],
                )
            start += size

    @pl.when(step == 0)
    def _():
        for copy in copies(0, 0):
            copy.start()

    @pl.when(step + 1 < steps)
    def _():
        for copy in copies(step + 1, (step + 1) % 2):
            copy.start()

    slot = step % 2
    for copy in copies(step, slot):
        copy.wait()
    pairs = jnp.concatenate([term[:, : 2 * half] for term in terms], axis=0)
    hidden = jnp.concatenate([term[:, 2 * half :] for term in terms], axis=0)
    both = dot(held[slot, 0], pairs, 0, 0).astype(BF16)
    gate_out[...] = both[:, :half]
    up_out[...] = both[:, half:]
    down_out[...] = dot(hidden, held[slot, 1], 0, 0).astype(BF16)


def weight_grads(rows, terms, width, half):
    groups = len(rows)
    total = sum(block.shape[0] for block in rows)
    tile = width // 2 if total <= 1024 else width // 8
    column = pl.BlockSpec((tile, half), lambda i: (i, 0))
    return pl.pallas_call(
        functools.partial(grads_body, groups, width, half),
        grid=(width // tile,),
        out_shape=[jax.ShapeDtypeStruct((width, half), BF16)] * 2
        + [jax.ShapeDtypeStruct((half, width), BF16)],
        in_specs=[pl.BlockSpec(memory_space=pl.ANY)] * groups
        + [pl.BlockSpec((term.shape[0], 3 * half), lambda i: (0, 0)) for term in terms],
        out_specs=[column, column, pl.BlockSpec((half, tile), lambda i: (0, i))],
        scratch_shapes=[
            pltpu.VMEM((2, 2, total, tile), BF16),
            pltpu.SemaphoreType.DMA((2, 2, groups)),
        ],
        compiler_params=pltpu.CompilerParams(vmem_limit_bytes=(22 if total <= 1024 else 48) * MIB),
        cost_estimate=pl.CostEstimate(
            flops=2 * 3 * total * width * half,
            bytes_accessed=4 * total * width + 6 * width * half,
            transcendentals=0,
        ),
        name="weight_grads",
    )(*rows, *terms)


def add(left, right):
    return (left.astype(F32) + right.astype(F32)).astype(BF16)


def local(tokens, upstream, expert_ids, gate_weights, w_gate, w_up, w_down):
    tok_count, width = tokens.shape
    half = w_gate.shape[1]
    count = lax.axis_size("expert")
    levels = count // (2 * PLANE)
    expert = (lax.axis_index("expert") // 2).astype(jnp.int32)[None]
    chosen = expert_ids[:, :, None] == jnp.arange(LANES, dtype=jnp.int32)[None, None, :]
    gates = jnp.sum(jnp.where(chosen, gate_weights.astype(F32)[:, :, None], 0.0), axis=1)
    home = jnp.concatenate([tokens, upstream, gates.astype(BF16)], axis=1)

    first, second, corner = first_route(count), second_route(count), corner_route(count)
    swap = core_route(count)
    onward, backward = level_route(count, 1), level_route(count, -1)
    both = jnp.concatenate([w_gate, w_up], axis=1)
    weights = [both, w_down, send(both, swap)]
    weights.append(send(w_down, swap))
    last = levels // 2
    groups = [(at, -at) if 0 < 2 * at < levels else (at,) for at in range(last + 1)]

    ways = {1: (home, None), -1: (home, None)}
    units, results, planes, arrived, far, rows, terms = [], [], {}, [], [], [], []
    done = ()
    for step in range(last + 4):
        ready, done, sent = done, [], ()

        def pass_on(block, pairs):
            result = send(after(block, *ready) if ready else block, pairs)
            done.append(result)
            return result

        if step <= last:
            here = [way for way in (1, -1) if step and ways[way][0] is not None]
            lists = [[ways[way][0] for way in here]]
            for way in here:
                if step + 1 < last or (way == 1 and step < last):
                    lists.append(list(ways[way]))
            lists = [blocks for blocks in lists if len(blocks) > 1]
            stacked = list(stacks(*lists)) if lists else []
            mine = home if step == 0 else stacked.pop(0) if len(here) > 1 else ways[1][0]
            new, corners = {1: (None, None), -1: (None, None)}, []
            for way in (1, -1):
                goes_on = step < last if way == 1 else step + 1 < last
                pairs = level_route(count, way)
                if step == 0:
                    if goes_on:
                        new[way] = (pass_on(home, pairs), None)
                elif way in here:
                    got = pass_on(stacked.pop(0) if goes_on else ways[way][1], pairs)
                    corner_at = tok_count if goes_on else 0
                    corners.append((got, corner_at, tok_count))
                    if goes_on:
                        new[way] = (got[:tok_count], got[tok_count:])
                    else:
                        new[way] = (None, got)
            sent = (mine,)
            beside = pass_on(mine, second)
            near = pass_on(mine if step else after(home, beside, *weights[2:]), first)
            if step == 0:
                across = send(beside, first)
                done.append(across)
                corners = [(across, 0, tok_count)]
                new = {way: (new[way][0], across) for way in new}
            own_blocks = [(ways[way][0], 0, tok_count) for way in here] or [(home, 0, tok_count)]
            units.append([own_blocks] + [[(block, 0, block.shape[0])] for block in (near, beside)] + [corners])
            ways = new
        if 1 <= step - 3 <= last:
            at = step - 3
            plane = sum(part.astype(F32) for part in planes[at]).astype(BF16)
            for i, shift in enumerate(groups[at]):
                piece = plane[i * tok_count : (i + 1) * tok_count]
                arrived.append(pass_on(piece, level_route(count, -shift)))
        if 0 <= step - 2 <= last:
            at = step - 2
            parts = results[at]
            planes[at] = [parts[0]]
            if at:
                planes[at].append(pass_on(parts[1], first))
                planes[at].append(pass_on(parts[2], second))
            if at == last:
                planes[at].append(pass_on(parts[3], corner))
            elif at:
                for i, shift in enumerate(groups[at]):
                    piece = parts[3][i * tok_count : (i + 1) * tok_count]
                    far.append(pass_on(piece, level_route(count, -shift)))
        if step == last + 3:
            far = sum(part.astype(F32) for part in (results[0][3], *far)).astype(BF16)
            arrived += [*planes[0], pass_on(results[0][1], first), pass_on(results[0][2], second), pass_on(far, corner)]
        if last + 1 < step:
            for at in range(last + 1) if step == last + 3 else ():
                block = rows[2 * at]
                if at == 0:
                    block = after(block, *planes[1][1:2])
                if at == last:
                    block = after(block, *planes[last][1:2])
                rows[2 * at + 1] = terms[2 * at + 1] = send(block, swap)
        if 0 <= step - 1 <= last:
            unit = units[step - 1]
            block, *span = unit[0][0]
            unit[0][0] = (after(block, *ready, *sent), *span)
            parts, own, kept = expert_terms(unit, weights, expert)
            done.append(parts[0])
            results.append(parts)
            rows += [kept, None]
            terms += [own, None]

    grads = weight_grads(rows, terms, width, half)
    arrived[-1] = after(arrived[-1], *grads)

    grad_tokens = sum(piece[:, :width].astype(F32) for piece in arrived).astype(BF16)
    gate_sums = sum(piece[:, width:].astype(F32) for piece in arrived)
    grad_gates = jnp.sum(jnp.where(chosen, gate_sums[:, None, :], 0.0), axis=2).astype(BF16)
    return (grad_tokens, grad_gates, *grads)


def solution(mesh):
    rows = P(("group", "expert"), None)
    return jax.shard_map(
        local,
        mesh=mesh,
        in_specs=(rows, rows, rows, rows, P("group", "expert"), P("group", "expert"), P("expert", "group")),
        out_specs=(rows, rows, P("group", "expert"), P("group", "expert"), P("expert", "group")),
        check_vma=False,
    )
```
